32 devices in a mesh: groups: 2 (over y), expert: 4 (over z), tensor: 4 (over x, core).
Axes of the slice: x: 2, y: 2, z: 4, core: 2. Of those that a mesh axis runs over, the one named last changes fastest.
Arguments:
- tokens: bfloat16 [1024, 4096], P(('groups', 'expert'), 'tensor'), parts along dimension 0, may hold values from -6 to 6
- expert_ids: int32 [1024, 2], P(('groups', 'expert')), parts along dimension 0, may hold values from 0 to 31, all different within a row; in each aligned block of 128 rows (0 to 127, 128 to 255, ...) at most 16 rows name the same one
- gate_values: float32 [1024, 2], P(('groups', 'expert')), parts along dimension 0, may hold values from 0.3 to 1
- teacher_out: float32 [1024, 4096], P(('groups', 'expert'), 'tensor'), parts along dimension 0, may hold values from -6 to 6
- student_gate: bfloat16 [64, 512, 4096], P('expert', 'tensor'), may hold values from -0.09375 to 0.09375
- student_up: bfloat16 [64, 512, 4096], P('expert', 'tensor'), may hold values from -0.09375 to 0.09375
- student_down: bfloat16 [64, 512, 4096], P('expert', None, 'tensor'), may hold values from -0.1875 to 0.1875
Outputs:
- student: float32 [1024, 4096], P(('groups', 'expert'), 'tensor'), parts along dimension 0
- residual: float32 [1024, 4096], P(('groups', 'expert'), 'tensor'), parts along dimension 0
The draws below stay inside these ranges and needn't reach their ends.
There are 2 independent parts, one for each index of `groups`. The reference program is written for one: setup_inputs(seed, part) draws one part's arguments, and reference() takes and returns one part's arrays. A program takes and returns all parts, laid end to end along the dimension named above; an argument that names none is the same for every part. Nothing has to cross between parts.
Inputs may be any that keep to these rules, and one draw needn't show every extreme that they name: `expert_ids`: each row names 2 different experts. In each aligned block of 128 rows (the rows of one index of expert) no expert is named by more than 16 rows, a bound that some block reaches.
All inputs are finite; a program needn't handle non-finite values.
Results may differ from the reference program's by a relative error of at most 0.0029.
Values may be sent and summed in bfloat16 or wider, within the bound.
A program may use at most 128 MiB of HBM per device.

```python
import math
import jax
import jax.numpy as jnp
import numpy as np
from jax import lax

D = 4096
EXPERTS = 32
EXP_HID = 1024
TOP = 2
TOK_DEV = 128
CAP = 16
SLAB_HID = 512
SLABS = 64
TOKENS = 512
N_EXPERT = 4


def steps_of(rng, dims, split, least, top_value):
    gain = 1.0
    for dim, shards_of in split:
        draws = jax.random.uniform(jax.random.fold_in(jax.random.fold_in(rng, 6), dim), (shards_of,), jnp.float32, least / len(split), top_value / len(split))
        gain = gain * jnp.repeat(jnp.exp(draws), dims[dim] // shards_of).reshape((-1,) + (1,) * (len(dims) - 1 - dim))
    return gain


def assign_block(key, own, number, rows, amount, top, limit, slope):
    sequence = jax.random.permutation(key, amount)
    packed, usual = shares(amount, rows * top, limit, slope, True), shares(amount, rows * top, limit, slope, False)
    places = jnp.arange(amount)

    def named(lengths, turn):
        used = int((lengths > 0).sum())
        fixed = max(1, used // 4)
        moved = fixed + (places - fixed + turn * (used - fixed)) % max(1, amount - fixed)
        return jnp.zeros((amount,), jnp.int32).at[sequence[jnp.where(places < fixed, places, moved)]].set(jnp.asarray(lengths, jnp.int32))

    lengths = jnp.where(number % 4 == 0, named(packed, number // 4), named(usual, number - number // 4 - 1))
    mixed = jax.random.permutation(jax.random.fold_in(own, 3), amount)
    giver, sink = mixed[0:amount // 2 * 2:2], mixed[1:amount // 2 * 2:2]
    room = jnp.minimum(lengths[giver] - 1, limit - lengths[sink]) // 2
    room = jnp.where((giver == sequence[0]) | (sink == sequence[0]) | (lengths[sink] == 0), 0, jnp.maximum(room, 0))
    moved = jax.random.randint(jax.random.fold_in(own, 4), (amount // 2,), 0, 1 << 20) % (room + 1)
    lengths = lengths.at[giver].add(-moved).at[sink].add(moved)
    members = jnp.searchsorted(jnp.cumsum(lengths), jnp.arange(rows * top), side="right").astype(jnp.int32)
    table = members.reshape(top, rows).T
    table = table[jax.random.permutation(jax.random.fold_in(own, 1), rows)]
    turn = jax.random.randint(jax.random.fold_in(own, 2), (rows, 1), 0, top)
    return jnp.take_along_axis(table, (jnp.arange(top)[None, :] + turn) % top, axis=1)


def shares(count, total, reach, lean, full):
    portions = [(1 << 20) // math.isqrt(rank ** lean) + 1 for rank in range(1, count + 1)]
    largest = reach if full else min(reach, max(-(-total // count), total * portions[0] // sum(portions)))
    least = 1 if total - largest >= count - 1 else 0
    given, rest = [largest] + [least] * (count - 1), total - largest - least * (count - 1)
    while rest > 0:
        free = [i for i in range(1, count) if given[i] < largest] or [i for i in range(1, count) if given[i] < reach]
        whole, left = sum([portions[i] for i in free]), rest
        for i in free:
            more = min(reach - given[i], max(1, left * portions[i] // whole), rest)
            given[i] = given[i] + more
            rest = rest - more
    return np.array(given)


def centred(key, shape, spread, limit, cuts=(), kind=jnp.bfloat16):
    drawn = spread * jax.random.normal(key, shape, jnp.float32)
    if cuts:
        drawn = drawn * steps_of(key, shape, cuts, -0.22, 0.18)
    return jnp.clip(drawn, -limit, limit).astype(kind)


def setup_inputs(seed: int = 0, part: int = 0) -> dict:
    arg_keys = jax.random.split(jax.random.key(seed), 8)
    part_keys = jax.random.split(jax.random.fold_in(arg_keys[7], part), 8)
    tokens = centred(part_keys[0], (TOKENS, D), 1.0, 6.0, ((0, 4), (1, 4)))
    expert_ids_keys = jax.random.split(jax.random.fold_in(part_keys[1], 1), TOKENS // TOK_DEV)
    expert_ids_turns = jax.random.permutation(jax.random.fold_in(part_keys[1], 3), TOKENS // TOK_DEV)
    expert_ids = jax.vmap(lambda own, number: assign_block(jax.random.fold_in(part_keys[1], 2), own, number, TOK_DEV, EXPERTS, TOP, CAP, 2))(expert_ids_keys, expert_ids_turns).reshape((TOKENS, TOP))
    gate_values = jnp.clip(0.3 + 0.7 * jax.random.uniform(part_keys[2], (TOKENS, TOP), jnp.float32) ** steps_of(part_keys[2], (TOKENS, TOP), ((0, 4),), -0.2, 0.2), 0.3, 1.0)
    teacher_out = centred(part_keys[3], (TOKENS, D), 1.0, 6.0, ((0, 4), (1, 4)), jnp.float32)
    student_gate = centred(arg_keys[4], (SLABS, SLAB_HID, D), D ** -0.5, 0.09375, ((0, 4), (1, 4)))
    student_up = centred(arg_keys[5], (SLABS, SLAB_HID, D), D ** -0.5, 0.09375, ((0, 4), (1, 4)))
    student_down = centred(arg_keys[6], (SLABS, SLAB_HID, D), EXP_HID ** -0.5, 0.1875, ((0, 4), (2, 4)))
    return {"tokens": tokens, "expert_ids": expert_ids, "gate_values": gate_values, "teacher_out": teacher_out, "student_gate": student_gate, "student_up": student_up, "student_down": student_down}


def reference(tokens, expert_ids, gate_values, teacher_out, student_gate, student_up, student_down):
    block_ids = expert_ids.reshape(N_EXPERT, TOK_DEV * TOP)
    onehot = (block_ids[:, :, None] == jnp.arange(EXPERTS, dtype=jnp.int32)[None, None, :]).astype(jnp.int32)
    earlier = (jnp.cumsum(onehot, axis=1) - onehot).astype(jnp.int32)
    position = jnp.sum(earlier * onehot, axis=2).astype(jnp.int32)
    block_index = jnp.arange(N_EXPERT, dtype=jnp.int32)[:, None]
    slot = (block_ids * (N_EXPERT * CAP) + block_index * CAP + position).reshape(-1).astype(jnp.int32)
    token_of = (jnp.arange(TOKENS * TOP, dtype=jnp.int32) // TOP).astype(jnp.int32)
    table = jnp.zeros((EXPERTS * N_EXPERT * CAP,), jnp.int32).at[slot].set(token_of)
    weight = jnp.zeros((EXPERTS * N_EXPERT * CAP,), jnp.float32).at[slot].set(gate_values.reshape(-1))
    table = table.reshape(EXPERTS, N_EXPERT * CAP)
    weight = weight.reshape(EXPERTS, N_EXPERT * CAP)
    gate_pairs = student_gate.reshape(EXPERTS, 2, SLAB_HID, D)
    up_pairs = student_up.reshape(EXPERTS, 2, SLAB_HID, D)
    down_pairs = student_down.reshape(EXPERTS, 2, SLAB_HID, D)

    def expert_step(running, items):
        rows_index, row_weight, gate_w, up_w, down_w = items
        picked = tokens[rows_index]
        halves = []
        for half in range(2):
            pre_gate = jnp.dot(picked, gate_w[half].T, preferred_element_type=jnp.float32)
            pre_up = jnp.dot(picked, up_w[half].T, preferred_element_type=jnp.float32)
            hidden = (jax.nn.silu(pre_gate) * pre_up).astype(jnp.bfloat16)
            halves.append(jnp.dot(hidden, down_w[half], preferred_element_type=jnp.float32))
        combined = halves[0] + halves[1]
        return running.at[rows_index].add(row_weight[:, None] * combined), None

    start_sum = jnp.zeros((TOKENS, D), jnp.float32)
    student, _ = lax.scan(expert_step, start_sum, (table, weight, gate_pairs, up_pairs, down_pairs))
    return student, teacher_out - student
```

```python
import functools
import jax
import jax.numpy as jnp
from jax import lax
from jax.experimental import pallas as pl
from jax.experimental.pallas import tpu as pltpu
from jax.sharding import PartitionSpec as P

EXPERTS = 32
TOP = 2
CAP = 16


def per_device(
    tokens, expert_ids, gate_values, teacher_out, student_gate, student_up, student_down
):
    row_count = tokens.shape[0]
    flat_ids = expert_ids.reshape(-1)
    onehot = (flat_ids[:, None] == jnp.arange(EXPERTS, dtype=jnp.int32)[None, :]).astype(jnp.int32)
    earlier = jnp.cumsum(onehot, axis=0) - onehot
    position = jnp.sum(earlier * onehot, axis=1)
    slot_ids = flat_ids * CAP + position
    slot_match = slot_ids[None, :] == jnp.arange(EXPERTS * CAP, dtype=jnp.int32)[:, None]
    picker = jnp.sum(
        slot_match.reshape(EXPERTS * CAP, row_count, TOP).astype(jnp.float32), axis=2
    ).astype(jnp.bfloat16)
    flat_gates = gate_values.reshape(-1)
    weighted = jnp.where(slot_match, flat_gates[None, :], jnp.zeros_like(flat_gates)[None, :])
    combiner = jnp.sum(weighted.reshape(EXPERTS * CAP, row_count, TOP), axis=2)
    width = tokens.shape[1]
    packed = jnp.dot(picker, tokens, preferred_element_type=jnp.float32).astype(jnp.bfloat16)
    doubled = jnp.broadcast_to(packed.reshape(EXPERTS, 1, CAP, width), (EXPERTS, 2, CAP, width))
    full_rows = lax.all_gather(
        lax.all_to_all(
            doubled.reshape(2 * EXPERTS, CAP, width),
            "expert",
            split_axis=0,
            concat_axis=0,
            tiled=True,
        ),
        "tensor",
        axis=2,
        tiled=True,
    )
    slab_local = student_gate.shape[0]
    source_count = full_rows.shape[0] // slab_local
    slot_count = full_rows.shape[1]
    grouped = full_rows.reshape(source_count, slab_local, slot_count, full_rows.shape[2])
    gate_pre = jnp.einsum(
        "nsid,shd->nsih", grouped, student_gate, preferred_element_type=jnp.float32
    )
    up_pre = jnp.einsum("nsid,shd->nsih", grouped, student_up, preferred_element_type=jnp.float32)
    activated = (jax.nn.silu(gate_pre) * up_pre).astype(jnp.bfloat16)
    whole_hidden = lax.all_gather(activated, "tensor", axis=3, tiled=True)
    outputs = jnp.einsum(
        "nsih,shd->nsid", whole_hidden, student_down, preferred_element_type=jnp.float32
    )
    flat_out = outputs.reshape(source_count * slab_local, slot_count, outputs.shape[3])
    returned_sum = lax.all_to_all(flat_out, "expert", split_axis=0, concat_axis=0, tiled=True)
    quarter_width = returned_sum.shape[2]
    halves_added = jnp.sum(returned_sum.reshape(EXPERTS, 2, CAP, quarter_width), axis=1).reshape(
        EXPERTS * CAP, quarter_width
    )
    student = lax.dot_general(
        combiner,
        halves_added,
        (((0,), (0,)), ((), ())),
        precision=lax.Precision.HIGHEST,
        preferred_element_type=jnp.float32,
    )
    return (student, teacher_out - student)


def fused_kernel(
    n, lead, lag, meta_ref, tok_ref, wg_ref, wu_ref, wd_ref, out_ref,
    wgu, wdb, gath, sids, packed, acc, hid, outs, back,
    wsem, dsem, zsend, zrecv, msend, mrecv, ssend, srecv, xsend, xrecv, fsend, frecv,
    hsend, hrecv, rsend, rrecv,
):
    z, t = lax.axis_index("expert"), lax.axis_index("tensor")
    sib = t + 1 - 2 * lax.rem(t, 2)
    across = lax.rem(t + 2, 4)
    order = (t, sib, across, lax.rem(sib + 2, 4))
    rows, kd = tok_ref.shape
    local, part = wg_ref.shape[0], wg_ref.shape[1]
    half = part // 2
    slots = local * CAP
    f32, bf16 = jnp.float32, jnp.bfloat16

    def remote(src, dst, send, recv, where):
        return pltpu.make_async_remote_copy(
            src_ref=src, dst_ref=dst, send_sem=send, recv_sem=recv,
            device_id=where, device_id_type=pl.DeviceIdType.MESH,
        )

    weight_copies = []
    for j in range(4):
        cols = pl.ds(pl.multiple_of(order[j] * kd, kd), kd)
        weight_copies.append((
            pltpu.make_async_copy(wg_ref.at[:, :, cols], wgu.at[j, :, 0:part, :], wsem.at[j, 0]),
            pltpu.make_async_copy(wu_ref.at[:, :, cols], wgu.at[j, :, part:2 * part, :], wsem.at[j, 1]),
        ))
    down_copies = []
    for j in range(4):
        for h in range(2):
            hrows = pl.ds(pl.multiple_of(order[j] * half, half), half)
            down_copies.append(pltpu.make_async_copy(
                wd_ref.at[:, h, hrows, :],
                wdb.at[:, pl.ds(j * part + h * half, half), :],
                dsem.at[j, h],
            ))
    for pair in weight_copies:
        for c in pair:
            c.start()
    for c in down_copies:
        c.start()

    barrier = pltpu.get_barrier_semaphore()
    peers = [{"expert": lax.rem(z + i, n)} for i in range(1, n)]
    peers += [{"tensor": order[j]} for j in range(1, 4)]
    for peer in peers:
        pl.semaphore_signal(barrier, inc=1, device_id=peer, device_id_type=pl.DeviceIdType.MESH)
    pl.semaphore_wait(barrier, len(peers))

    def tok_copy(d, src, own):
        ref = tok_ref if own else gath.at[src]
        return remote(ref, gath.at[src], zsend.at[d, src], zrecv.at[src], {"expert": z + 1 - 2 * d})

    def sid_copy(d, src):
        return remote(sids.at[src], sids.at[src], msend.at[d, src], mrecv.at[src], {"expert": z + 1 - 2 * d})

    def each_way(fn):
        @pl.when(z < n - 1)
        def _():
            fn(0)

        @pl.when(z > 0)
        def _():
            fn(1)

    each_way(lambda d: tok_copy(d, z, True).start())

    id0, id1 = meta_ref[0:1, :], meta_ref[1:2, :]
    names = lax.broadcasted_iota(jnp.int32, (n * local, rows), 0).astype(f32)
    hit0, hit1 = names == id0, names == id1
    hits = (jnp.where(hit0, 1.0, 0.0) + jnp.where(hit1, 1.0, 0.0)).astype(bf16)
    before = jnp.where(
        lax.broadcasted_iota(jnp.int32, (rows, rows), 0) < lax.broadcasted_iota(jnp.int32, (rows, rows), 1),
        1.0, 0.0,
    ).astype(bf16)
    earlier = jnp.dot(hits, before, preferred_element_type=f32)
    sid0 = id0 * CAP + jnp.sum(jnp.where(hit0, earlier, 0.0), axis=0, keepdims=True)
    sid1 = id1 * CAP + jnp.sum(jnp.where(hit1, earlier, 0.0), axis=0, keepdims=True)
    line = lax.broadcasted_iota(jnp.int32, (8, rows), 0)
    sids[z] = jnp.where(line == 0, sid0, jnp.where(line == 1, sid1, 0.0))
    each_way(lambda d: sid_copy(d, z).start())

    slot_names = lax.broadcasted_iota(jnp.int32, (slots, rows), 0)

    def sib_copy(src):
        return remote(packed.at[0, src], packed.at[1, src], ssend.at[src], srecv.at[src], {"tensor": sib})

    def across_copy(src):
        return remote(packed.at[0, src], packed.at[2, src], xsend.at[src], xrecv.at[src], {"tensor": across})

    def onward_copy(src):
        return remote(packed.at[2, src], packed.at[3, src], fsend.at[src], frecv.at[src], {"tensor": sib})

    def pick(src, own):
        mine = (slot_names + z * slots).astype(f32)
        a, b = sids[src, 0:1, :], sids[src, 1:2, :]
        picker = (jnp.where(mine == a, 1.0, 0.0) + jnp.where(mine == b, 1.0, 0.0)).astype(bf16)
        toks = tok_ref[...] if own else gath[src]
        got = jnp.dot(picker, toks, preferred_element_type=f32).astype(bf16)
        packed[0, src] = got.reshape(local, CAP, kd)
        across_copy(src).start()
        sib_copy(src).start()

    def at_step(k, fn):
        if k == 0:
            fn(z, None)
            return

        @pl.when(z >= k)
        def _():
            fn(z - k, 0)

        @pl.when(z + k < n)
        def _():
            fn(z + k, 1)

    def can_forward(d):
        return z < n - 1 if d == 0 else z > 0

    def arrive(src, d):
        tok_copy(d, src, False).wait_recv()
        sid_copy(d, src).wait_recv()

        @pl.when(can_forward(d))
        def _():
            tok_copy(d, src, False).start()
            sid_copy(d, src).start()

        pick(src, False)

    def onward(src, d):
        across_copy(src).wait_recv()
        onward_copy(src).start()

    pick(z, True)
    for k in range(1, n):
        at_step(k, arrive)
        if k >= 2:
            at_step(k - 2, onward)

    nt = (((1,), (1,)), ((), ()))

    def rows_of(j, e):
        return packed[j, :, e].reshape(n * CAP, kd)

    def partial(j, e):
        return lax.dot_general(rows_of(j, e), wgu[j, e], nt, preferred_element_type=f32)

    for s in range(n):
        sib_copy(s).wait_recv()
    for j in range(2):
        for c in weight_copies[j]:
            c.wait()

    def first(e, carry):
        acc[e] = partial(0, e) + partial(1, e)
        return carry

    lax.fori_loop(0, local, first, 0)

    for k in range(max(n - 2, 0), n):
        at_step(k, onward)
    for s in range(n):
        onward_copy(s).wait_recv()
    for j in range(2, 4):
        for c in weight_copies[j]:
            c.wait()
    for c in down_copies:
        c.wait()

    def hid_sib(e):
        return remote(hid.at[e, :, 0:part], hid.at[e, :, part:2 * part], hsend.at[0, e], hrecv.at[0, e], {"tensor": sib})

    def hid_across(e):
        return remote(hid.at[e, :, 0:part], hid.at[e, :, 2 * part:3 * part], hsend.at[1, e], hrecv.at[1, e], {"tensor": across})

    def hid_onward(e):
        return remote(hid.at[e, :, 2 * part:3 * part], hid.at[e, :, 3 * part:4 * part], hsend.at[2, e], hrecv.at[2, e], {"tensor": sib})

    def ret_copy(i, e):
        to = lax.rem(z + i, n)
        return remote(outs.at[e, to], back.at[z, e], rsend.at[i, e], rrecv.at[z, e], {"expert": to})

    def second(i, carry):
        @pl.when(i < local)
        def _():
            pre = acc[i] + partial(2, i) + partial(3, i)
            gate, up = pre[:, :part], pre[:, part:]
            hid[i, :, 0:part] = (gate / (1.0 + jnp.exp(-gate)) * up).astype(bf16)
            hid_across(i).start()
            hid_sib(i).start()

        @pl.when((i >= lead) & (i < local + lead))
        def _():
            hid_across(i - lead).wait_recv()
            hid_onward(i - lead).start()

        @pl.when(i >= lag)
        def _():
            e = i - lag
            hid_sib(e).wait_recv()
            hid_onward(e).wait_recv()
            got = jnp.dot(hid[e], wdb[e], preferred_element_type=f32).astype(bf16)
            outs[e] = got.reshape(n, CAP, kd)
            for step in range(1, n):
                ret_copy(step, e).start()

        return carry

    lax.fori_loop(0, local + lag, second, 0)

    sid0, sid1 = sids[z, 0:1, :], sids[z, 1:2, :]
    g0, g1 = meta_ref[2:3, :], meta_ref[3:4, :]
    for i in range(n):
        frm = lax.rem(z + i, n)
        if i == 0:
            got = outs[:, z].reshape(slots, kd)
        else:
            for e in range(local):
                remote(outs.at[e, z], back.at[frm, e], rsend.at[i, e], rrecv.at[frm, e], {"expert": frm}).wait_recv()
            got = back[frm].reshape(slots, kd)
        mine = (slot_names + frm * slots).astype(f32)
        spread = (jnp.where(mine == sid0, g0, 0.0) + jnp.where(mine == sid1, g1, 0.0)).T
        high = spread.astype(bf16)
        low = (spread - high.astype(f32)).astype(bf16)
        term = jnp.dot(high, got, preferred_element_type=f32) + jnp.dot(low, got, preferred_element_type=f32)
        out_ref[...] = term if i == 0 else out_ref[...] + term

    each_way(lambda d: tok_copy(d, z, True).wait_send())
    each_way(lambda d: sid_copy(d, z).wait_send())

    def left(src, d):
        @pl.when(can_forward(d))
        def _():
            tok_copy(d, src, False).wait_send()
            sid_copy(d, src).wait_send()

    for k in range(1, n):
        at_step(k, left)
    for s in range(n):
        sib_copy(s).wait_send()
        across_copy(s).wait_send()
        onward_copy(s).wait_send()
    for e in range(local):
        hid_sib(e).wait_send()
        hid_across(e).wait_send()
        hid_onward(e).wait_send()
        for step in range(1, n):
            ret_copy(step, e).wait_send()


def fused_device(
    n, tokens, expert_ids, gate_values, teacher_out, student_gate, student_up, student_down
):
    rows, kd = tokens.shape
    slabs, half, full = student_gate.shape
    local, part = slabs // 2, 2 * half
    meta = jnp.concatenate(
        [expert_ids.T.astype(jnp.float32), gate_values.T, jnp.zeros((4, rows), jnp.float32)], axis=0
    )
    wg = student_gate.reshape(local, part, full)
    wu = student_up.reshape(local, part, full)
    wd = student_down.reshape(local, 2, student_down.shape[1], kd)
    bf16, f32 = jnp.bfloat16, jnp.float32
    dma = pltpu.SemaphoreType.DMA
    vmem = pl.BlockSpec(memory_space=pltpu.VMEM)
    hbm = pl.BlockSpec(memory_space=pl.ANY)
    student = pl.pallas_call(
        functools.partial(fused_kernel, n, 2, 4),
        out_shape=jax.ShapeDtypeStruct((rows, kd), f32),
        in_specs=[vmem, vmem, hbm, hbm, hbm],
        out_specs=vmem,
        scratch_shapes=[
            pltpu.VMEM((4, local, 2 * part, kd), bf16),
            pltpu.VMEM((local, 4 * part, kd), bf16),
            pltpu.VMEM((n, rows, kd), bf16),
            pltpu.VMEM((n, 8, rows), f32),
            pltpu.VMEM((4, n, local, CAP, kd), bf16),
            pltpu.VMEM((local, n * CAP, 2 * part), f32),
            pltpu.VMEM((local, n * CAP, 4 * part), bf16),
            pltpu.VMEM((local, n, CAP, kd), bf16),
            pltpu.VMEM((n, local, CAP, kd), bf16),
            dma((4, 2)), dma((4, 2)), dma((2, n)), dma((n,)), dma((2, n)), dma((n,)),
            dma((n,)), dma((n,)), dma((n,)), dma((n,)), dma((n,)), dma((n,)),
            dma((3, local)), dma((3, local)), dma((n, local)), dma((n, local)),
        ],
        compiler_params=pltpu.CompilerParams(
            collective_id=0, has_side_effects=True, vmem_limit_bytes=63 * 1024 * 1024
        ),
        cost_estimate=pl.CostEstimate(
            flops=6 * local * n * CAP * 2 * part * full, bytes_accessed=6 * slabs * half * full,
            transcendentals=0,
        ),
    )(meta, tokens, wg, wu, wd)
    return (student, teacher_out - student)


def solution(mesh):
    in_specs = (
        P(("groups", "expert"), "tensor"),
        P(("groups", "expert"), None),
        P(("groups", "expert"), None),
        P(("groups", "expert"), "tensor"),
        P("expert", "tensor", None),
        P("expert", "tensor", None),
        P("expert", None, "tensor"),
    )
    out_specs = (P(("groups", "expert"), "tensor"), P(("groups", "expert"), "tensor"))
    sizes = dict(mesh.shape)
    fused = sizes["tensor"] == 4 and 2 * sizes["expert"] <= EXPERTS // 2 and sizes["expert"] == 4
    body = functools.partial(fused_device, sizes["expert"]) if fused else per_device
    return jax.shard_map(
        body, mesh=mesh, in_specs=in_specs, out_specs=out_specs, check_vma=False
    )
```

```python
import functools
import jax
import jax.numpy as jnp
from jax import lax
from jax.experimental import pallas as pl
from jax.experimental.pallas import tpu as pltpu
from jax.sharding import PartitionSpec as P

EXPERTS = 32
TOP = 2
CAP = 16


def per_device(
    tokens, expert_ids, gate_values, teacher_out, student_gate, student_up, student_down
):
    row_count = tokens.shape[0]
    flat_ids = expert_ids.reshape(-1)
    onehot = (flat_ids[:, None] == jnp.arange(EXPERTS, dtype=jnp.int32)[None, :]).astype(jnp.int32)
    earlier = jnp.cumsum(onehot, axis=0) - onehot
    position = jnp.sum(earlier * onehot, axis=1)
    slot_ids = flat_ids * CAP + position
    slot_match = slot_ids[None, :] == jnp.arange(EXPERTS * CAP, dtype=jnp.int32)[:, None]
    picker = jnp.sum(
        slot_match.reshape(EXPERTS * CAP, row_count, TOP).astype(jnp.float32), axis=2
    ).astype(jnp.bfloat16)
    flat_gates = gate_values.reshape(-1)
    weighted = jnp.where(slot_match, flat_gates[None, :], jnp.zeros_like(flat_gates)[None, :])
    combiner = jnp.sum(weighted.reshape(EXPERTS * CAP, row_count, TOP), axis=2)
    width = tokens.shape[1]
    packed = jnp.dot(picker, tokens, preferred_element_type=jnp.float32).astype(jnp.bfloat16)
    doubled = jnp.broadcast_to(packed.reshape(EXPERTS, 1, CAP, width), (EXPERTS, 2, CAP, width))
    full_rows = lax.all_gather(
        lax.all_to_all(
            doubled.reshape(2 * EXPERTS, CAP, width),
            "expert",
            split_axis=0,
            concat_axis=0,
            tiled=True,
        ),
        "tensor",
        axis=2,
        tiled=True,
    )
    slab_local = student_gate.shape[0]
    source_count = full_rows.shape[0] // slab_local
    slot_count = full_rows.shape[1]
    grouped = full_rows.reshape(source_count, slab_local, slot_count, full_rows.shape[2])
    gate_pre = jnp.einsum(
        "nsid,shd->nsih", grouped, student_gate, preferred_element_type=jnp.float32
    )
    up_pre = jnp.einsum("nsid,shd->nsih", grouped, student_up, preferred_element_type=jnp.float32)
    activated = (jax.nn.silu(gate_pre) * up_pre).astype(jnp.bfloat16)
    whole_hidden = lax.all_gather(activated, "tensor", axis=3, tiled=True)
    outputs = jnp.einsum(
        "nsih,shd->nsid", whole_hidden, student_down, preferred_element_type=jnp.float32
    )
    flat_out = outputs.reshape(source_count * slab_local, slot_count, outputs.shape[3])
    returned_sum = lax.all_to_all(flat_out, "expert", split_axis=0, concat_axis=0, tiled=True)
    quarter_width = returned_sum.shape[2]
    halves_added = jnp.sum(returned_sum.reshape(EXPERTS, 2, CAP, quarter_width), axis=1).reshape(
        EXPERTS * CAP, quarter_width
    )
    student = lax.dot_general(
        combiner,
        halves_added,
        (((0,), (0,)), ((), ())),
        precision=lax.Precision.HIGHEST,
        preferred_element_type=jnp.float32,
    )
    return (student, teacher_out - student)


def fused_kernel(
    n, lead, lag, ids_ref, gates_ref, tok_ref, wg_ref, wu_ref, wd_ref, out_ref,
    wgu, wdb, gath, sids, packed, acc, hid, outs, back,
    wsem, dsem, zsend, zrecv, msend, mrecv, ssend, srecv, xsend, xrecv, fsend, frecv,
    hsend, hrecv, rsend, rrecv,
):
    z, t = lax.axis_index("expert"), lax.axis_index("tensor")
    sib = t + 1 - 2 * lax.rem(t, 2)
    across = lax.rem(t + 2, 4)
    order = (t, sib, across, lax.rem(sib + 2, 4))
    rows, kd = tok_ref.shape
    local, part = wg_ref.shape[0], wg_ref.shape[1]
    half = part // 2
    slots = local * CAP
    parts, cd = gath.shape[1], gath.shape[3]
    f32, bf16 = jnp.float32, jnp.bfloat16

    def remote(src, dst, send, recv, where):
        return pltpu.make_async_remote_copy(
            src_ref=src, dst_ref=dst, send_sem=send, recv_sem=recv,
            device_id=where, device_id_type=pl.DeviceIdType.MESH,
        )

    weight_copies = []
    for j in range(4):
        cols = pl.ds(pl.multiple_of(order[j] * kd, kd), kd)
        weight_copies.append((
            pltpu.make_async_copy(wg_ref.at[:, :, cols], wgu.at[j, :, 0:part, :], wsem.at[j, 0]),
            pltpu.make_async_copy(wu_ref.at[:, :, cols], wgu.at[j, :, part:2 * part, :], wsem.at[j, 1]),
        ))
    down_copies = []
    for j in range(4):
        for h in range(2):
            hrows = pl.ds(pl.multiple_of(order[j] * half, half), half)
            down_copies.append(pltpu.make_async_copy(
                wd_ref.at[:, h, hrows, :],
                wdb.at[:, pl.ds(j * part + h * half, half), :],
                dsem.at[j, h],
            ))
    for pair in weight_copies:
        for c in pair:
            c.start()
    for c in down_copies:
        c.start()

    barrier = pltpu.get_barrier_semaphore()
    peers = [{"expert": lax.rem(z + i, n)} for i in range(1, n)]
    peers += [{"tensor": order[j]} for j in range(1, 4)]
    for peer in peers:
        pl.semaphore_signal(barrier, inc=1, device_id=peer, device_id_type=pl.DeviceIdType.MESH)
    pl.semaphore_wait(barrier, len(peers))

    def tok_copy(d, c, src, own):
        ref = tok_ref.at[:, c * cd:(c + 1) * cd] if own else gath.at[src, c]
        return remote(ref, gath.at[src, c], zsend.at[d, c, src], zrecv.at[c, src], {"expert": z + 1 - 2 * d})

    def sid_copy(d, src):
        return remote(sids.at[src], sids.at[src], msend.at[d, src], mrecv.at[src], {"expert": z + 1 - 2 * d})

    def each_way(fn):
        @pl.when(z < n - 1)
        def _():
            fn(0)

        @pl.when(z > 0)
        def _():
            fn(1)

    each_way(lambda d: tok_copy(d, 0, z, True).start())

    id0, id1 = ids_ref[0:1, :].astype(f32), ids_ref[1:2, :].astype(f32)
    names = lax.broadcasted_iota(jnp.int32, (n * local, rows), 0).astype(f32)
    hit0, hit1 = names == id0, names == id1
    hits = (jnp.where(hit0, 1.0, 0.0) + jnp.where(hit1, 1.0, 0.0)).astype(bf16)
    before = jnp.where(
        lax.broadcasted_iota(jnp.int32, (rows, rows), 0) < lax.broadcasted_iota(jnp.int32, (rows, rows), 1),
        1.0, 0.0,
    ).astype(bf16)
    earlier = jnp.dot(hits, before, preferred_element_type=f32)
    sid0 = id0 * CAP + jnp.sum(jnp.where(hit0, earlier, 0.0), axis=0, keepdims=True)
    sid1 = id1 * CAP + jnp.sum(jnp.where(hit1, earlier, 0.0), axis=0, keepdims=True)
    line = lax.broadcasted_iota(jnp.int32, (8, rows), 0)
    sids[z] = jnp.where(line == 0, sid0, jnp.where(line == 1, sid1, 0.0))
    each_way(lambda d: sid_copy(d, z).start())

    slot_names = lax.broadcasted_iota(jnp.int32, (slots, rows), 0)

    def sib_copy(c, src):
        return remote(packed.at[0, c, src], packed.at[1, c, src], ssend.at[c, src], srecv.at[c, src], {"tensor": sib})

    def across_copy(c, src):
        return remote(packed.at[0, c, src], packed.at[2, c, src], xsend.at[c, src], xrecv.at[c, src], {"tensor": across})

    def onward_copy(c, src):
        return remote(packed.at[2, c, src], packed.at[3, c, src], fsend.at[c, src], frecv.at[c, src], {"tensor": sib})

    def pick(c, src, own):
        mine = (slot_names + z * slots).astype(f32)
        a, b = sids[src, 0:1, :], sids[src, 1:2, :]
        picker = (jnp.where(mine == a, 1.0, 0.0) + jnp.where(mine == b, 1.0, 0.0)).astype(bf16)
        toks = tok_ref[:, c * cd:(c + 1) * cd] if own else gath[src, c]
        got = jnp.dot(picker, toks, preferred_element_type=f32).astype(bf16)
        packed[0, c, src] = got.reshape(local, CAP, cd)
        across_copy(c, src).start()
        sib_copy(c, src).start()

    def at_step(k, fn, c):
        if k == 0:
            fn(c, z, None)
            return

        @pl.when(z >= k)
        def _():
            fn(c, z - k, 0)

        @pl.when(z + k < n)
        def _():
            fn(c, z + k, 1)

    def can_forward(d):
        return z < n - 1 if d == 0 else z > 0

    def arrive(c, src, d):
        tok_copy(d, c, src, False).wait_recv()
        if c == 0:
            sid_copy(d, src).wait_recv()

        @pl.when(can_forward(d))
        def _():
            tok_copy(d, c, src, False).start()
            if c == 0:
                sid_copy(d, src).start()

        pick(c, src, False)

    def onward(c, src, d):
        across_copy(c, src).wait_recv()
        onward_copy(c, src).start()

    nt = (((1,), (1,)), ((), ()))

    def partial(c, e):
        total = None
        for j in range(4):
            term = lax.dot_general(
                packed[j, c, :, e].reshape(n * CAP, cd), wgu[j, e, :, c * cd:(c + 1) * cd],
                nt, preferred_element_type=f32,
            )
            total = term if total is None else total + term
        return total

    def settle(c):
        for s in range(n):
            sib_copy(c, s).wait_recv()
            onward_copy(c, s).wait_recv()

    def early(c):
        def run(e, carry):
            acc[e] = partial(c, e) if c == 0 else acc[e] + partial(c, e)
            return carry

        lax.fori_loop(0, local, run, 0)

    pick(0, z, True)
    for k in range(1, n):
        at_step(k, arrive, 0)
        if k == 1:
            for c in range(1, parts):
                each_way(lambda d: tok_copy(d, c, z, True).start())
                pick(c, z, True)
        if k >= 2:
            at_step(k - 2, onward, 0)
    behind = [(0, n - 2), (0, n - 1)]
    for c in range(1, parts):
        behind.append((c, 0))
        for k in range(1, n):
            at_step(k, arrive, c)
            at_step(behind[0][1], onward, behind[0][0])
            behind = behind[1:] + [(c, k)]
    for pair in weight_copies:
        for w in pair:
            w.wait()
    for c in range(parts - 1):
        while behind and behind[0][0] == c:
            at_step(behind[0][1], onward, c)
            behind = behind[1:]
        settle(c)
        early(c)
    for c, k in behind:
        at_step(k, onward, c)
    settle(parts - 1)
    for w in down_copies:
        w.wait()

    def hid_sib(e):
        return remote(hid.at[e, :, 0:part], hid.at[e, :, part:2 * part], hsend.at[0, e], hrecv.at[0, e], {"tensor": sib})

    def hid_across(e):
        return remote(hid.at[e, :, 0:part], hid.at[e, :, 2 * part:3 * part], hsend.at[1, e], hrecv.at[1, e], {"tensor": across})

    def hid_onward(e):
        return remote(hid.at[e, :, 2 * part:3 * part], hid.at[e, :, 3 * part:4 * part], hsend.at[2, e], hrecv.at[2, e], {"tensor": sib})

    def ret_copy(i, e):
        to = lax.rem(z + i, n)
        return remote(outs.at[e, to], back.at[z, e], rsend.at[i, e], rrecv.at[z, e], {"expert": to})

    def second(i, carry):
        @pl.when(i < local)
        def _():
            pre = acc[i] + partial(parts - 1, i)
            gate, up = pre[:, :part], pre[:, part:]
            hid[i, :, 0:part] = (gate / (1.0 + jnp.exp(-gate)) * up).astype(bf16)
            hid_across(i).start()
            hid_sib(i).start()

        @pl.when((i >= lead) & (i < local + lead))
        def _():
            hid_across(i - lead).wait_recv()
            hid_onward(i - lead).start()

        @pl.when(i >= lag)
        def _():
            e = i - lag
            hid_sib(e).wait_recv()
            hid_onward(e).wait_recv()
            got = jnp.dot(hid[e], wdb[e], preferred_element_type=f32).astype(bf16)
            outs[e] = got.reshape(n, CAP, kd)
            back[z, e] = outs[e, z]
            for step in range(1, n):
                ret_copy(step, e).start()

        return carry

    lax.fori_loop(0, local + lag, second, 0)

    sid0, sid1 = sids[z, 0:1, :], sids[z, 1:2, :]
    g0, g1 = gates_ref[0:1, :], gates_ref[1:2, :]
    cuts = (0, max(local - 2, 1), local)
    for lo, hi in zip(cuts[:-1], cuts[1:]):
        for i in range(1, n):
            frm = lax.rem(z + i, n)
            for e in range(lo, hi):
                remote(outs.at[e, z], back.at[frm, e], rsend.at[i, e], rrecv.at[frm, e], {"expert": frm}).wait_recv()
        size = (hi - lo) * CAP
        got = back[:, lo:hi].reshape(n * size, kd)
        ramp = lax.broadcasted_iota(jnp.int32, (size, rows), 0)
        mine = jnp.concatenate([ramp + (s * slots + lo * CAP) for s in range(n)], axis=0).astype(f32)
        spread = (jnp.where(mine == sid0, g0, 0.0) + jnp.where(mine == sid1, g1, 0.0)).T
        high = spread.astype(bf16)
        low = (spread - high.astype(f32)).astype(bf16)
        term = jnp.dot(high, got, preferred_element_type=f32) + jnp.dot(low, got, preferred_element_type=f32)
        out_ref[...] = term if lo == 0 else out_ref[...] + term

    for c in range(parts):
        each_way(lambda d: tok_copy(d, c, z, True).wait_send())
    each_way(lambda d: sid_copy(d, z).wait_send())

    def left(c, src, d):
        @pl.when(can_forward(d))
        def _():
            tok_copy(d, c, src, False).wait_send()
            if c == 0:
                sid_copy(d, src).wait_send()

    for c in range(parts):
        for k in range(1, n):
            at_step(k, left, c)
        for s in range(n):
            sib_copy(c, s).wait_send()
            across_copy(c, s).wait_send()
            onward_copy(c, s).wait_send()
    for e in range(local):
        hid_sib(e).wait_send()
        hid_across(e).wait_send()
        hid_onward(e).wait_send()
        for step in range(1, n):
            ret_copy(step, e).wait_send()


def finish_kernel(student_ref, teacher_ref, out_ref, residual_ref):
    out_ref[...] = student_ref[...]
    residual_ref[...] = teacher_ref[...] - student_ref[...]


def fused_device(
    n, tokens, expert_ids, gate_values, teacher_out, student_gate, student_up, student_down
):
    rows, kd = tokens.shape
    slabs, half, full = student_gate.shape
    local, part = slabs // 2, 2 * half
    parts = 2
    wg = student_gate.reshape(local, part, full)
    wu = student_up.reshape(local, part, full)
    wd = student_down.reshape(local, 2, student_down.shape[1], kd)
    bf16, f32 = jnp.bfloat16, jnp.float32
    dma = pltpu.SemaphoreType.DMA
    vmem = pl.BlockSpec(memory_space=pltpu.VMEM)
    hbm = pl.BlockSpec(memory_space=pl.ANY)
    student = pl.pallas_call(
        functools.partial(fused_kernel, n, 2, 4),
        out_shape=jax.ShapeDtypeStruct((rows, kd), f32),
        in_specs=[vmem, vmem, vmem, hbm, hbm, hbm],
        out_specs=vmem,
        scratch_shapes=[
            pltpu.VMEM((4, local, 2 * part, kd), bf16),
            pltpu.VMEM((local, 4 * part, kd), bf16),
            pltpu.VMEM((n, parts, rows, kd // parts), bf16),
            pltpu.VMEM((n, 8, rows), f32),
            pltpu.VMEM((4, parts, n, local, CAP, kd // parts), bf16),
            pltpu.VMEM((local, n * CAP, 2 * part), f32),
            pltpu.VMEM((local, n * CAP, 4 * part), bf16),
            pltpu.VMEM((local, n, CAP, kd), bf16),
            pltpu.VMEM((n, local, CAP, kd), bf16),
            dma((4, 2)), dma((4, 2)), dma((2, parts, n)), dma((parts, n)), dma((2, n)), dma((n,)),
            dma((parts, n)), dma((parts, n)), dma((parts, n)), dma((parts, n)), dma((parts, n)), dma((parts, n)),
            dma((3, local)), dma((3, local)), dma((n, local)), dma((n, local)),
        ],
        compiler_params=pltpu.CompilerParams(
            collective_id=0, has_side_effects=True, vmem_limit_bytes=63 * 1024 * 1024
        ),
        cost_estimate=pl.CostEstimate(
            flops=6 * local * n * CAP * 2 * part * full, bytes_accessed=6 * slabs * half * full,
            transcendentals=0,
        ),
    )(expert_ids.T, gate_values.T, tokens, wg, wu, wd)
    block = pl.BlockSpec((rows // 2, kd), lambda i: (i, 0))
    return tuple(pl.pallas_call(
        finish_kernel,
        grid=(2,),
        out_shape=[jax.ShapeDtypeStruct((rows, kd), f32)] * 2,
        in_specs=[block, block],
        out_specs=[block, block],
    )(student, teacher_out))


def solution(mesh):
    in_specs = (
        P(("groups", "expert"), "tensor"),
        P(("groups", "expert"), None),
        P(("groups", "expert"), None),
        P(("groups", "expert"), "tensor"),
        P("expert", "tensor", None),
        P("expert", "tensor", None),
        P("expert", None, "tensor"),
    )
    out_specs = (P(("groups", "expert"), "tensor"), P(("groups", "expert"), "tensor"))
    sizes = dict(mesh.shape)
    fused = sizes["tensor"] == 4 and 2 * sizes["expert"] <= EXPERTS // 2 and sizes["expert"] == 4
    body = functools.partial(fused_device, sizes["expert"]) if fused else per_device
    return jax.shard_map(
        body, mesh=mesh, in_specs=in_specs, out_specs=out_specs, check_vma=False
    )
```

```python
import functools
import jax
import jax.numpy as jnp
from jax import lax
from jax.experimental import pallas as pl
from jax.experimental.pallas import tpu as pltpu
from jax.sharding import PartitionSpec as P

EXPERTS = 32
TOP = 2
CAP = 16


def per_device(
    tokens, expert_ids, gate_values, teacher_out, student_gate, student_up, student_down
):
    row_count = tokens.shape[0]
    flat_ids = expert_ids.reshape(-1)
    onehot = (flat_ids[:, None] == jnp.arange(EXPERTS, dtype=jnp.int32)[None, :]).astype(jnp.int32)
    earlier = jnp.cumsum(onehot, axis=0) - onehot
    position = jnp.sum(earlier * onehot, axis=1)
    slot_ids = flat_ids * CAP + position
    slot_match = slot_ids[None, :] == jnp.arange(EXPERTS * CAP, dtype=jnp.int32)[:, None]
    picker = jnp.sum(
        slot_match.reshape(EXPERTS * CAP, row_count, TOP).astype(jnp.float32), axis=2
    ).astype(jnp.bfloat16)
    flat_gates = gate_values.reshape(-1)
    weighted = jnp.where(slot_match, flat_gates[None, :], jnp.zeros_like(flat_gates)[None, :])
    combiner = jnp.sum(weighted.reshape(EXPERTS * CAP, row_count, TOP), axis=2)
    width = tokens.shape[1]
    packed = jnp.dot(picker, tokens, preferred_element_type=jnp.float32).astype(jnp.bfloat16)
    doubled = jnp.broadcast_to(packed.reshape(EXPERTS, 1, CAP, width), (EXPERTS, 2, CAP, width))
    full_rows = lax.all_gather(
        lax.all_to_all(
            doubled.reshape(2 * EXPERTS, CAP, width),
            "expert",
            split_axis=0,
            concat_axis=0,
            tiled=True,
        ),
        "tensor",
        axis=2,
        tiled=True,
    )
    slab_local = student_gate.shape[0]
    source_count = full_rows.shape[0] // slab_local
    slot_count = full_rows.shape[1]
    grouped = full_rows.reshape(source_count, slab_local, slot_count, full_rows.shape[2])
    gate_pre = jnp.einsum(
        "nsid,shd->nsih", grouped, student_gate, preferred_element_type=jnp.float32
    )
    up_pre = jnp.einsum("nsid,shd->nsih", grouped, student_up, preferred_element_type=jnp.float32)
    activated = (jax.nn.silu(gate_pre) * up_pre).astype(jnp.bfloat16)
    whole_hidden = lax.all_gather(activated, "tensor", axis=3, tiled=True)
    outputs = jnp.einsum(
        "nsih,shd->nsid", whole_hidden, student_down, preferred_element_type=jnp.float32
    )
    flat_out = outputs.reshape(source_count * slab_local, slot_count, outputs.shape[3])
    returned_sum = lax.all_to_all(flat_out, "expert", split_axis=0, concat_axis=0, tiled=True)
    quarter_width = returned_sum.shape[2]
    halves_added = jnp.sum(returned_sum.reshape(EXPERTS, 2, CAP, quarter_width), axis=1).reshape(
        EXPERTS * CAP, quarter_width
    )
    student = lax.dot_general(
        combiner,
        halves_added,
        (((0,), (0,)), ((), ())),
        precision=lax.Precision.HIGHEST,
        preferred_element_type=jnp.float32,
    )
    return (student, teacher_out - student)


def fused_kernel(
    n, lead, lag, ids_ref, gates_ref, tok_ref, wg_ref, wu_ref, wd_ref, out_ref,
    wgu, wdb, gath, sids, packed, acc, hid, outs, back,
    wsem, dsem, zsend, zrecv, msend, mrecv, ssend, srecv, xsend, xrecv, fsend, frecv,
    hsend, hrecv, rsend, rrecv,
):
    z, t = lax.axis_index("expert"), lax.axis_index("tensor")
    sib = t + 1 - 2 * lax.rem(t, 2)
    across = lax.rem(t + 2, 4)
    order = (t, sib, across, lax.rem(sib + 2, 4))
    rows, kd = tok_ref.shape
    local, part = wg_ref.shape[0], wg_ref.shape[1]
    half = part // 2
    slots = local * CAP
    parts, cd = gath.shape[1], gath.shape[3]
    f32, bf16 = jnp.float32, jnp.bfloat16

    def remote(src, dst, send, recv, where):
        return pltpu.make_async_remote_copy(
            src_ref=src, dst_ref=dst, send_sem=send, recv_sem=recv,
            device_id=where, device_id_type=pl.DeviceIdType.MESH,
        )

    weight_copies = []
    for j in range(4):
        cols = pl.ds(pl.multiple_of(order[j] * kd, kd), kd)
        weight_copies.append((
            pltpu.make_async_copy(wg_ref.at[:, :, cols], wgu.at[j, :, 0:part, :], wsem.at[j, 0]),
            pltpu.make_async_copy(wu_ref.at[:, :, cols], wgu.at[j, :, part:2 * part, :], wsem.at[j, 1]),
        ))
    down_copies = []
    for j in range(4):
        for h in range(2):
            hrows = pl.ds(pl.multiple_of(order[j] * half, half), half)
            down_copies.append(pltpu.make_async_copy(
                wd_ref.at[:, h, hrows, :],
                wdb.at[:, pl.ds(j * part + h * half, half), :],
                dsem.at[j, h],
            ))
    for pair in weight_copies:
        for c in pair:
            c.start()
    for c in down_copies:
        c.start()

    barrier = pltpu.get_barrier_semaphore()
    peers = [{"expert": lax.rem(z + i, n)} for i in range(1, n)]
    peers += [{"tensor": order[j]} for j in range(1, 4)]
    for peer in peers:
        pl.semaphore_signal(barrier, inc=1, device_id=peer, device_id_type=pl.DeviceIdType.MESH)
    pl.semaphore_wait(barrier, len(peers))

    def tok_copy(d, c, src, own):
        ref = tok_ref.at[:, c * cd:(c + 1) * cd] if own else gath.at[src, c]
        return remote(ref, gath.at[src, c], zsend.at[d, c, src], zrecv.at[c, src], {"expert": z + 1 - 2 * d})

    def sid_copy(d, src):
        return remote(sids.at[src], sids.at[src], msend.at[d, src], mrecv.at[src], {"expert": z + 1 - 2 * d})

    def each_way(fn):
        @pl.when(z < n - 1)
        def _():
            fn(0)

        @pl.when(z > 0)
        def _():
            fn(1)

    each_way(lambda d: tok_copy(d, 0, z, True).start())

    id0, id1 = ids_ref[0:1, :].astype(f32), ids_ref[1:2, :].astype(f32)
    names = lax.broadcasted_iota(jnp.int32, (n * local, rows), 0).astype(f32)
    hit0, hit1 = names == id0, names == id1
    hits = (jnp.where(hit0, 1.0, 0.0) + jnp.where(hit1, 1.0, 0.0)).astype(bf16)
    before = jnp.where(
        lax.broadcasted_iota(jnp.int32, (rows, rows), 0) < lax.broadcasted_iota(jnp.int32, (rows, rows), 1),
        1.0, 0.0,
    ).astype(bf16)
    earlier = jnp.dot(hits, before, preferred_element_type=f32)
    sid0 = id0 * CAP + jnp.sum(jnp.where(hit0, earlier, 0.0), axis=0, keepdims=True)
    sid1 = id1 * CAP + jnp.sum(jnp.where(hit1, earlier, 0.0), axis=0, keepdims=True)
    line = lax.broadcasted_iota(jnp.int32, (8, rows), 0)
    sids[z] = jnp.where(line == 0, sid0, jnp.where(line == 1, sid1, 0.0))
    each_way(lambda d: sid_copy(d, z).start())

    slot_names = lax.broadcasted_iota(jnp.int32, (slots, rows), 0)

    def sib_copy(c, src):
        return remote(packed.at[0, c, src], packed.at[1, c, src], ssend.at[c, src], srecv.at[c, src], {"tensor": sib})

    def across_copy(c, src):
        return remote(packed.at[0, c, src], packed.at[2, c, src], xsend.at[c, src], xrecv.at[c, src], {"tensor": across})

    def onward_copy(c, src):
        return remote(packed.at[2, c, src], packed.at[3, c, src], fsend.at[c, src], frecv.at[c, src], {"tensor": sib})

    def pick(c, src, own):
        mine = (slot_names + z * slots).astype(f32)
        a, b = sids[src, 0:1, :], sids[src, 1:2, :]
        picker = (jnp.where(mine == a, 1.0, 0.0) + jnp.where(mine == b, 1.0, 0.0)).astype(bf16)
        toks = tok_ref[:, c * cd:(c + 1) * cd] if own else gath[src, c]
        got = jnp.dot(picker, toks, preferred_element_type=f32).astype(bf16)
        packed[0, c, src] = got.reshape(local, CAP, cd)
        across_copy(c, src).start()
        sib_copy(c, src).start()

    def at_step(k, fn, c):
        if k == 0:
            fn(c, z, None)
            return

        @pl.when(z >= k)
        def _():
            fn(c, z - k, 0)

        @pl.when(z + k < n)
        def _():
            fn(c, z + k, 1)

    def can_forward(d):
        return z < n - 1 if d == 0 else z > 0

    def arrive(c, src, d):
        tok_copy(d, c, src, False).wait_recv()
        if c == 0:
            sid_copy(d, src).wait_recv()

        @pl.when(can_forward(d))
        def _():
            tok_copy(d, c, src, False).start()
            if c == 0:
                sid_copy(d, src).start()

        pick(c, src, False)

    def onward(c, src, d):
        across_copy(c, src).wait_recv()
        onward_copy(c, src).start()

    nt = (((1,), (1,)), ((), ()))

    def partial(c, e):
        total = None
        for j in range(4):
            term = lax.dot_general(
                packed[j, c, :, e].reshape(n * CAP, cd), wgu[j, e, :, c * cd:(c + 1) * cd],
                nt, preferred_element_type=f32,
            )
            total = term if total is None else total + term
        return total

    def settle(c):
        for s in range(n):
            sib_copy(c, s).wait_recv()
            onward_copy(c, s).wait_recv()

    def early(c):
        def run(e, carry):
            acc[e] = partial(c, e) if c == 0 else acc[e] + partial(c, e)
            return carry

        lax.fori_loop(0, local, run, 0)

    pick(0, z, True)
    for c in range(1, parts):
        each_way(lambda d: tok_copy(d, c, z, True).start())
        pick(c, z, True)
    for k in range(1, n):
        at_step(k, arrive, 0)
        if k >= 2:
            at_step(k - 2, onward, 0)
    behind = [(0, n - 2), (0, n - 1)]
    for c in range(1, parts):
        behind.append((c, 0))
        for k in range(1, n):
            at_step(k, arrive, c)
            at_step(behind[0][1], onward, behind[0][0])
            behind = behind[1:] + [(c, k)]
    for pair in weight_copies:
        for w in pair:
            w.wait()
    for c in range(parts - 1):
        while behind and behind[0][0] == c:
            at_step(behind[0][1], onward, c)
            behind = behind[1:]
        settle(c)
        early(c)
    for c, k in behind:
        at_step(k, onward, c)
    settle(parts - 1)
    for w in down_copies:
        w.wait()

    def hid_sib(e):
        return remote(hid.at[e, :, 0:part], hid.at[e, :, part:2 * part], hsend.at[0, e], hrecv.at[0, e], {"tensor": sib})

    def hid_across(e):
        return remote(hid.at[e, :, 0:part], hid.at[e, :, 2 * part:3 * part], hsend.at[1, e], hrecv.at[1, e], {"tensor": across})

    def hid_onward(e):
        return remote(hid.at[e, :, 2 * part:3 * part], hid.at[e, :, 3 * part:4 * part], hsend.at[2, e], hrecv.at[2, e], {"tensor": sib})

    def ret_copy(i, e):
        to = lax.rem(z + i, n)
        return remote(outs.at[e, to], back.at[z, e], rsend.at[i, e], rrecv.at[z, e], {"expert": to})

    def second(i, carry):
        @pl.when(i < local)
        def _():
            pre = acc[i] + partial(parts - 1, i)
            gate, up = pre[:, :part], pre[:, part:]
            hid[i, :, 0:part] = (gate / (1.0 + jnp.exp(-gate)) * up).astype(bf16)
            hid_across(i).start()
            hid_sib(i).start()

        @pl.when((i >= lead) & (i < local + lead))
        def _():
            hid_across(i - lead).wait_recv()
            hid_onward(i - lead).start()

        @pl.when(i >= lag)
        def _():
            e = i - lag
            hid_sib(e).wait_recv()
            hid_onward(e).wait_recv()
            got = jnp.dot(hid[e], wdb[e], preferred_element_type=f32).astype(bf16)
            outs[e] = got.reshape(n, CAP, kd)
            back[z, e] = outs[e, z]
            for step in range(1, n):
                ret_copy(step, e).start()

        return carry

    lax.fori_loop(0, local + lag, second, 0)

    sid0, sid1 = sids[z, 0:1, :], sids[z, 1:2, :]
    g0, g1 = gates_ref[0:1, :], gates_ref[1:2, :]
    cuts = (0, max(local - 2, 1), local)
    for lo, hi in zip(cuts[:-1], cuts[1:]):
        for i in range(1, n):
            frm = lax.rem(z + i, n)
            for e in range(lo, hi):
                remote(outs.at[e, z], back.at[frm, e], rsend.at[i, e], rrecv.at[frm, e], {"expert": frm}).wait_recv()
        size = (hi - lo) * CAP
        got = back[:, lo:hi].reshape(n * size, kd)
        ramp = lax.broadcasted_iota(jnp.int32, (size, rows), 0)
        mine = jnp.concatenate([ramp + (s * slots + lo * CAP) for s in range(n)], axis=0).astype(f32)
        spread = (jnp.where(mine == sid0, g0, 0.0) + jnp.where(mine == sid1, g1, 0.0)).T
        high = spread.astype(bf16)
        low = (spread - high.astype(f32)).astype(bf16)
        term = jnp.dot(high, got, preferred_element_type=f32) + jnp.dot(low, got, preferred_element_type=f32)
        out_ref[...] = term if lo == 0 else out_ref[...] + term

    for c in range(parts):
        each_way(lambda d: tok_copy(d, c, z, True).wait_send())
    each_way(lambda d: sid_copy(d, z).wait_send())

    def left(c, src, d):
        @pl.when(can_forward(d))
        def _():
            tok_copy(d, c, src, False).wait_send()
            if c == 0:
                sid_copy(d, src).wait_send()

    for c in range(parts):
        for k in range(1, n):
            at_step(k, left, c)
        for s in range(n):
            sib_copy(c, s).wait_send()
            across_copy(c, s).wait_send()
            onward_copy(c, s).wait_send()
    for e in range(local):
        hid_sib(e).wait_send()
        hid_across(e).wait_send()
        hid_onward(e).wait_send()
        for step in range(1, n):
            ret_copy(step, e).wait_send()


def finish_kernel(student_ref, teacher_ref, out_ref, residual_ref):
    out_ref[...] = student_ref[...]
    residual_ref[...] = teacher_ref[...] - student_ref[...]


def fused_device(
    n, tokens, expert_ids, gate_values, teacher_out, student_gate, student_up, student_down
):
    rows, kd = tokens.shape
    slabs, half, full = student_gate.shape
    local, part = slabs // 2, 2 * half
    parts = 2
    wg = student_gate.reshape(local, part, full)
    wu = student_up.reshape(local, part, full)
    wd = student_down.reshape(local, 2, student_down.shape[1], kd)
    bf16, f32 = jnp.bfloat16, jnp.float32
    dma = pltpu.SemaphoreType.DMA
    vmem = pl.BlockSpec(memory_space=pltpu.VMEM)
    hbm = pl.BlockSpec(memory_space=pl.ANY)
    student = pl.pallas_call(
        functools.partial(fused_kernel, n, 2, 4),
        out_shape=jax.ShapeDtypeStruct((rows, kd), f32),
        in_specs=[vmem, vmem, vmem, hbm, hbm, hbm],
        out_specs=vmem,
        scratch_shapes=[
            pltpu.VMEM((4, local, 2 * part, kd), bf16),
            pltpu.VMEM((local, 4 * part, kd), bf16),
            pltpu.VMEM((n, parts, rows, kd // parts), bf16),
            pltpu.VMEM((n, 8, rows), f32),
            pltpu.VMEM((4, parts, n, local, CAP, kd // parts), bf16),
            pltpu.VMEM((local, n * CAP, 2 * part), f32),
            pltpu.VMEM((local, n * CAP, 4 * part), bf16),
            pltpu.VMEM((local, n, CAP, kd), bf16),
            pltpu.VMEM((n, local, CAP, kd), bf16),
            dma((4, 2)), dma((4, 2)), dma((2, parts, n)), dma((parts, n)), dma((2, n)), dma((n,)),
            dma((parts, n)), dma((parts, n)), dma((parts, n)), dma((parts, n)), dma((parts, n)), dma((parts, n)),
            dma((3, local)), dma((3, local)), dma((n, local)), dma((n, local)),
        ],
        compiler_params=pltpu.CompilerParams(
            collective_id=0, has_side_effects=True, vmem_limit_bytes=63 * 1024 * 1024
        ),
        cost_estimate=pl.CostEstimate(
            flops=6 * local * n * CAP * 2 * part * full, bytes_accessed=6 * slabs * half * full,
            transcendentals=0,
        ),
    )(expert_ids.T, gate_values.T, tokens, wg, wu, wd)
    block = pl.BlockSpec((rows // 2, kd), lambda i: (i, 0))
    return tuple(pl.pallas_call(
        finish_kernel,
        grid=(2,),
        out_shape=[jax.ShapeDtypeStruct((rows, kd), f32)] * 2,
        in_specs=[block, block],
        out_specs=[block, block],
    )(student, teacher_out))


def solution(mesh):
    in_specs = (
        P(("groups", "expert"), "tensor"),
        P(("groups", "expert"), None),
        P(("groups", "expert"), None),
        P(("groups", "expert"), "tensor"),
        P("expert", "tensor", None),
        P("expert", "tensor", None),
        P("expert", None, "tensor"),
    )
    out_specs = (P(("groups", "expert"), "tensor"), P(("groups", "expert"), "tensor"))
    sizes = dict(mesh.shape)
    fused = sizes["tensor"] == 4 and 2 * sizes["expert"] <= EXPERTS // 2 and sizes["expert"] == 4
    body = functools.partial(fused_device, sizes["expert"]) if fused else per_device
    return jax.shard_map(
        body, mesh=mesh, in_specs=in_specs, out_specs=out_specs, check_vma=False
    )
```
